32 devices in a mesh: sa: 8 (over y, x, core), sb: 4 (over z).
Axes of the slice: x: 2, y: 2, z: 4, core: 2. Of those that a mesh axis runs over, the one named last changes fastest.
Arguments:
- spectra: bfloat16 [131072, 1024], P(('sa', 'sb')), as said below
- omega: int32 [1024, 256], replicated, may hold values from -4 to 4
Outputs:
- basis: bfloat16 [131072, 256], P(('sa', 'sb'))
- projected: float32 [256, 1024], replicated
The draws below stay inside these ranges and needn't reach their ends.
Inputs may be any that keep to these rules, and one draw needn't show every extreme that they name: `spectra`: rows are full rank over the features.
All inputs are finite; a program needn't handle non-finite values.
Results may differ from the reference program's by a relative error of at most 0.002.
Values sent between devices are 32-bit elements; how exact they have to be, the bound alone decides.
A program may use at most 64 MiB of HBM per device.

```python
import jax
import jax.numpy as jnp
from jax import lax

F = 1024
K = 256
ROWS = 131072


def draw_spectra(key, part):
    key = jax.random.fold_in(key, 11)
    first, second, third = jax.random.split(key, 3)
    position = jnp.arange(ROWS, dtype=jnp.float32)
    ramp = 1.0 + 2.0 * position / ROWS
    row_scale = jnp.exp(jax.random.uniform(second, (ROWS, 1), jnp.float32) * jnp.log(10.0))
    col_scale = 0.1 * jnp.exp(jax.random.uniform(third, (1, F), jnp.float32) * jnp.log(10.0))
    base = jax.random.normal(first, (ROWS, F), jnp.float32)
    return (base * row_scale * ramp[:, None] * col_scale).astype(jnp.bfloat16)


def touch_ends(values, own_key, low, high):
    dims = values.shape
    index_at = [jax.random.randint(jax.random.fold_in(own_key, axis), (), 0, dims[axis]) for axis in range(len(dims))]
    values = values.at[tuple(index_at)].set(low)
    longest = dims.index(max(dims))
    index_at[longest] = (index_at[longest] + 1) % dims[longest]
    return values.at[tuple(index_at)].set(high)


def setup_inputs(seed: int = 0) -> dict:
    key_list = jax.random.split(jax.random.key(seed), 3)
    return {
        "spectra": draw_spectra(jax.random.fold_in(key_list[2], 71), 0),
        "omega": touch_ends(jax.random.randint(key_list[1], (F, K), -4, 5), jax.random.fold_in(key_list[1], 1), -4, 4).astype(jnp.int32),
    }


def reference(spectra, omega):
    gain = (3.0 / (20.0 * F)) ** 0.5
    sketch = jnp.dot(spectra.astype(jnp.float32), omega.astype(jnp.bfloat16).astype(jnp.float32), preferred_element_type=jnp.float32) * gain
    gram = jnp.dot(sketch.T.astype(jnp.float32), sketch.astype(jnp.float32), precision=lax.Precision.HIGHEST, preferred_element_type=jnp.float32)
    lower = jnp.linalg.cholesky(gram)
    inverse = jax.scipy.linalg.solve_triangular(lower, jnp.eye(K, dtype=jnp.float32), lower=True)
    basis = (jnp.dot(sketch.astype(jnp.float32), inverse.T.astype(jnp.float32), precision=lax.Precision.HIGHEST, preferred_element_type=jnp.float32) * jnp.sqrt(jnp.float32(ROWS))).astype(jnp.bfloat16)
    projected = jnp.dot(basis.T.astype(jnp.float32), spectra.astype(jnp.float32), preferred_element_type=jnp.float32) / ROWS
    return (basis, projected)
```

```python
import functools

import jax
import jax.numpy as jnp
from jax import lax
from jax.experimental import pallas as pl
from jax.experimental.pallas import tpu as pltpu
from jax.sharding import PartitionSpec as P

F32 = jnp.float32
BF16 = jnp.bfloat16
PANEL = 32
LEAF = 8
CHUNK = 512
COLS = 256


def dot(a, b, ca=1, cb=0):
    return lax.dot_general(a, b, (((ca,), (cb,)), ((), ())), preferred_element_type=F32)


def split2(a):
    high = a.astype(BF16)
    return high, (a - high.astype(F32)).astype(BF16)


def split3(a):
    high, rest = a.astype(BF16), None
    rest = a - high.astype(F32)
    mid = rest.astype(BF16)
    return high, mid, (rest - mid.astype(F32)).astype(BF16)


def dot_f32(a, b):
    a1, a2, a3 = split3(a)
    b1, b2, b3 = split3(b)
    return dot(
        jnp.concatenate([a1, a1, a1, a2, a2, a3], axis=1),
        jnp.concatenate([b1, b2, b3, b1, b2, b1], axis=0),
    )


def rank_update(u, v):
    a1, a2, a3 = split3(u)
    b1, b2, b3 = split3(v)
    return dot(
        jnp.concatenate([a1, a1, a1, a2, a2, a3], axis=0),
        jnp.concatenate([b1, b2, b3, b1, b2, b1], axis=0),
        0,
        0,
    )


def leaf_inverse(block, first):
    a = {}
    for j in range(LEAF):
        column = jnp.broadcast_to(block[:, first + j : first + j + 1], (LEAF, 128))
        for i in range(j, LEAF):
            a[i, j] = jnp.broadcast_to(column[i : i + 1, :], (LEAF, 128))
    low, inv = {}, {}
    for j in range(LEAF):
        inv[j, j] = lax.rsqrt(a[j, j])
        for i in range(j + 1, LEAF):
            low[i, j] = a[i, j] * inv[j, j]
        for k in range(j + 1, LEAF):
            for i in range(k, LEAF):
                a[i, k] = a[i, k] - low[i, j] * low[k, j]
    for j in range(LEAF):
        for i in range(j + 1, LEAF):
            total = low[i, j] * inv[j, j]
            for k in range(j + 1, i):
                total = total + low[i, k] * inv[k, j]
            inv[i, j] = -total * inv[i, i]
    return inv


def factor_panel(block):
    sub = lax.broadcasted_iota(jnp.int32, (LEAF, 128), 0)
    tiles = [block[LEAF * q : LEAF * (q + 1), :] for q in range(PANEL // LEAF)]
    count = len(tiles)
    for q in range(count):
        inv = leaf_inverse(tiles[q], LEAF * q)
        scaled = jnp.zeros((LEAF, 128), F32)
        for j in range(LEAF):
            column = inv[LEAF - 1, j]
            for i in range(LEAF - 2, j - 1, -1):
                column = jnp.where(sub == i, inv[i, j], column)
            if j:
                column = jnp.where(sub < j, 0.0, column)
            scaled = scaled + column * jnp.broadcast_to(tiles[q][j : j + 1, :], (LEAF, 128))
        raw = {}
        for s in range(q + 1, count):
            for j in range(LEAF):
                lane = LEAF * q + j
                raw[s, j] = jnp.broadcast_to(tiles[s][:, lane : lane + 1], (LEAF, 128))
        for s in range(q + 1, count):
            value = tiles[s]
            for j in range(LEAF):
                factor = raw[s, 0] * inv[j, 0]
                for k in range(1, j + 1):
                    factor = factor + raw[s, k] * inv[j, k]
                value = value - factor * jnp.broadcast_to(scaled[j : j + 1, :], (LEAF, 128))
            tiles[s] = value
        tiles[q] = scaled
    return jnp.concatenate(tiles, axis=0)


def factor_step(k, work, inverse):
    rank = work.shape[0]
    rows = pl.ds(pl.multiple_of(k * PANEL, PANEL), PANEL)
    panel = work[rows, :]
    turned = pltpu.roll(panel[:, :rank], lax.rem(rank - k * PANEL, rank), 1)[:, :128]
    lane = lax.broadcasted_iota(jnp.int32, (PANEL, 128), 1)
    sub = lax.broadcasted_iota(jnp.int32, (PANEL, 128), 0)
    block = jnp.where(lane < PANEL, turned, jnp.where(lane == sub + PANEL, 1.0, 0.0))
    small = factor_panel(block)[:, PANEL : 2 * PANEL]
    done = dot_f32(small, panel)
    inverse[rows, :] = done[:, rank:]
    work[...] = work[...] - rank_update(done[:, :rank], done)


def factor_init(gram, work):
    rank = gram.shape[0]
    sub = lax.broadcasted_iota(jnp.int32, (rank, rank), 0)
    lane = lax.broadcasted_iota(jnp.int32, (rank, rank), 1)
    work[:, :rank] = gram
    work[:, rank:] = jnp.where(sub == lane, 1.0, 0.0)


def kernel(
    n_sa, n_sb,
    x_hbm, omega_ref, basis_ref, proj_ref,
    x_v, hi_v, lo_v, hit_v, lot_v, om_v, hh_v, hl_v, gram_v, cross_v,
    gbuf, zbuf, gfull, cbuf, cpart, czbuf, cfull, work, inverse,
    x_sem, send_sem, recv_sem,
):
    rows, features = x_hbm.shape
    rank = omega_ref.shape[1]
    share = rank // n_sa
    per_tile = n_sb // (share // 8)
    width = features // per_tile
    total_rows = rows * n_sa * n_sb
    gain = (3.0 / (20.0 * features)) ** 0.5
    chunks = rows // CHUNK
    a_me, b_me = lax.axis_index("sa"), lax.axis_index("sb")

    def x_copy(i):
        part = pl.ds(pl.multiple_of(i * CHUNK, CHUNK), CHUNK)
        return pltpu.make_async_copy(x_hbm.at[part], x_v.at[part], x_sem.at[i])

    for i in range(chunks):
        x_copy(i).start()

    def start(phase, axis, count, me, source, target):
        copies = []
        for p in range(1, count):
            peer = lax.rem(me + p, count)
            copy = pltpu.make_async_remote_copy(
                src_ref=source(peer),
                dst_ref=target,
                send_sem=send_sem.at[phase, p],
                recv_sem=recv_sem.at[phase, p],
                device_id={axis: peer},
                device_id_type=pl.DeviceIdType.MESH,
            )
            copy.start()
            copies.append(copy)
        return copies

    def finish(copies):
        for copy in copies:
            copy.wait()

    barrier = pltpu.get_barrier_semaphore()
    for p in range(1, n_sa):
        pl.semaphore_signal(
            barrier, inc=1, device_id={"sa": lax.rem(a_me + p, n_sa)}, device_id_type=pl.DeviceIdType.MESH
        )
    for p in range(1, n_sb):
        pl.semaphore_signal(
            barrier, inc=1, device_id={"sb": lax.rem(b_me + p, n_sb)}, device_id_type=pl.DeviceIdType.MESH
        )

    om_v[...] = omega_ref[...].astype(F32).astype(BF16)
    hh_v[...] = jnp.zeros_like(hh_v)
    hl_v[...] = jnp.zeros_like(hl_v)

    @pl.loop(0, chunks)
    def _(i):
        x_copy(i).wait()
        part = pl.ds(pl.multiple_of(i * CHUNK, CHUNK), CHUNK)
        sketch = dot(x_v[part, :], om_v[...]) * gain
        hi, lo = split2(sketch)
        hi_t, lo_t = split2(sketch.T)
        hi_v[part, :] = hi
        lo_v[part, :] = lo
        hit_v[:, part] = hi_t
        lot_v[:, part] = lo_t
        hh_v[...] += dot(hi_t, hi)
        hl_v[...] += dot(hi_t, lo)

    cut = lambda i: pl.ds(pl.multiple_of(i * share, share), share)
    gram_v[...] = hh_v[...] + (hl_v[...] + hl_v[...].T)

    pl.semaphore_wait(barrier, n_sa - 1 + n_sb - 1)
    copies = start(0, "sa", n_sa, a_me, lambda t: gram_v.at[cut(t)], gbuf.at[a_me])
    gbuf[a_me] = gram_v[cut(a_me), :]

    def cross(begin, end):
        @pl.loop(begin, end)
        def _(i):
            block = pl.ds(pl.multiple_of(i * COLS, COLS), COLS)
            x = x_v[:, block]
            cross_v[:, block] = dot(hit_v[...], x) + dot(lot_v[...], x)

    blocks = features // COLS
    cross(0, blocks // 2)

    def total(buffer, count):
        value = buffer[0]
        for i in range(1, count):
            value = value + buffer[i]
        return value

    finish(copies)
    zbuf[b_me] = total(gbuf, n_sa)
    copies = start(1, "sb", n_sb, b_me, lambda t: zbuf.at[b_me], zbuf.at[b_me])
    cross(blocks // 2, blocks)
    finish(copies)
    gfull[cut(a_me), :] = total(zbuf, n_sb)
    copies = start(2, "sa", n_sa, a_me, lambda t: gfull.at[cut(a_me)], gfull.at[cut(a_me)])
    c_copies = start(3, "sa", n_sa, a_me, lambda t: cross_v.at[cut(t)], cbuf.at[a_me])
    cbuf[a_me] = cross_v[cut(a_me), :]
    finish(copies)

    factor_init(gfull[...], work)
    panels = rank // PANEL

    def factor(begin, end):
        @pl.loop(begin, end)
        def _(k):
            factor_step(k, work, inverse)

    def piece(t, first):
        return (
            pl.ds(pl.multiple_of(first + lax.div(t, per_tile) * 8, 8), 8),
            pl.ds(pl.multiple_of(lax.rem(t, per_tile) * width, width), width),
        )

    factor(0, panels * 3 // 8)
    finish(c_copies)
    cpart[...] = total(cbuf, n_sa)
    copies = start(4, "sb", n_sb, b_me, lambda t: cpart.at[piece(t, 0)], czbuf.at[b_me])
    czbuf[b_me] = cpart[piece(b_me, 0)]
    factor(panels * 3 // 8, panels * 5 // 8)
    finish(copies)
    mine = piece(b_me, a_me * share)
    cfull[mine] = total(czbuf, n_sb)
    copies = start(5, "sb", n_sb, b_me, lambda t: cfull.at[mine], cfull.at[mine])
    factor(panels * 5 // 8, panels * 7 // 8)
    finish(copies)
    copies = start(6, "sa", n_sa, a_me, lambda t: cfull.at[cut(a_me)], cfull.at[cut(a_me)])
    factor(panels * 7 // 8, panels)

    inv_hi, inv_lo = split2(inverse[...])
    root = float(total_rows) ** 0.5

    @pl.loop(0, chunks)
    def _(i):
        part = pl.ds(pl.multiple_of(i * CHUNK, CHUNK), CHUNK)
        hi = hi_v[part, :]
        value = dot(hi, inv_hi, 1, 1) + (dot(hi, inv_lo, 1, 1) + dot(lo_v[part, :], inv_hi, 1, 1))
        basis_ref[part, :] = (value * root).astype(BF16)

    finish(copies)
    scale = root / total_rows

    @pl.loop(0, blocks)
    def _(i):
        block = pl.ds(pl.multiple_of(i * COLS, COLS), COLS)
        hi, lo = split2(cfull[:, block])
        proj_ref[:, block] = (dot(inv_hi, hi) + (dot(inv_hi, lo) + dot(inv_lo, hi))) * scale


def on_device(spectra, omega):
    rows, features = spectra.shape
    rank = omega.shape[1]
    n_sa, n_sb = lax.axis_size("sa"), lax.axis_size("sb")
    share = rank // n_sa
    width = features * (share // 8) // n_sb
    vmem = pltpu.VMEM
    return pl.pallas_call(
        functools.partial(kernel, n_sa, n_sb),
        out_shape=(
            jax.ShapeDtypeStruct((rows, rank), BF16),
            jax.ShapeDtypeStruct((rank, features), F32),
        ),
        in_specs=[pl.BlockSpec(memory_space=pl.ANY), pl.BlockSpec(memory_space=pltpu.VMEM)],
        out_specs=(pl.BlockSpec(memory_space=pltpu.VMEM), pl.BlockSpec(memory_space=pltpu.VMEM)),
        scratch_shapes=[
            vmem((rows, features), BF16),
            vmem((rows, rank), BF16),
            vmem((rows, rank), BF16),
            vmem((rank, rows), BF16),
            vmem((rank, rows), BF16),
            vmem((features, rank), BF16),
            vmem((rank, rank), F32),
            vmem((rank, rank), F32),
            vmem((rank, rank), F32),
            vmem((rank, features), F32),
            vmem((n_sa, share, rank), F32),
            vmem((n_sb, share, rank), F32),
            vmem((rank, rank), F32),
            vmem((n_sa, share, features), F32),
            vmem((share, features), F32),
            vmem((n_sb, 8, width), F32),
            vmem((rank, features), F32),
            vmem((rank, 2 * rank), F32),
            vmem((rank, rank), F32),
            pltpu.SemaphoreType.DMA((rows // CHUNK,)),
            pltpu.SemaphoreType.DMA((7, max(n_sa, n_sb))),
            pltpu.SemaphoreType.DMA((7, max(n_sa, n_sb))),
        ],
        compiler_params=pltpu.CompilerParams(
            collective_id=0, has_side_effects=True, vmem_limit_bytes=52 * 2**20
        ),
    )(spectra, omega)


def solution(mesh):
    return jax.shard_map(
        on_device,
        mesh=mesh,
        in_specs=(P(("sa", "sb"), None), P()),
        out_specs=(P(("sa", "sb"), None), P()),
        check_vma=False,
    )
```

```python
import functools

import jax
import jax.numpy as jnp
from jax import lax
from jax.experimental import pallas as pl
from jax.experimental.pallas import tpu as pltpu
from jax.sharding import PartitionSpec as P

F32 = jnp.float32
BF16 = jnp.bfloat16
PANEL = 32
LEAF = 8
CHUNK = 512
COLS = 256


def dot(a, b, ca=1, cb=0):
    return lax.dot_general(a, b, (((ca,), (cb,)), ((), ())), preferred_element_type=F32)


def split2(a):
    high = a.astype(BF16)
    return high, (a - high.astype(F32)).astype(BF16)


def split3(a):
    high, rest = a.astype(BF16), None
    rest = a - high.astype(F32)
    mid = rest.astype(BF16)
    return high, mid, (rest - mid.astype(F32)).astype(BF16)


def dot_f32(a, b):
    a1, a2, a3 = split3(a)
    b1, b2, b3 = split3(b)
    return dot(
        jnp.concatenate([a1, a1, a1, a2, a2, a3], axis=1),
        jnp.concatenate([b1, b2, b3, b1, b2, b1], axis=0),
    )


def rank_update(u, v):
    a1, a2, a3 = split3(u)
    b1, b2, b3 = split3(v)
    return dot(
        jnp.concatenate([a1, a1, a1, a2, a2, a3], axis=0),
        jnp.concatenate([b1, b2, b3, b1, b2, b1], axis=0),
        0,
        0,
    )


def leaf_inverse(block, first):
    a = {}
    for j in range(LEAF):
        column = jnp.broadcast_to(block[:, first + j : first + j + 1], (LEAF, 128))
        for i in range(j, LEAF):
            a[i, j] = jnp.broadcast_to(column[i : i + 1, :], (LEAF, 128))
    low, inv = {}, {}
    for j in range(LEAF):
        inv[j, j] = lax.rsqrt(a[j, j])
        for i in range(j + 1, LEAF):
            low[i, j] = a[i, j] * inv[j, j]
        for k in range(j + 1, LEAF):
            for i in range(k, LEAF):
                a[i, k] = a[i, k] - low[i, j] * low[k, j]
    for j in range(LEAF):
        for i in range(j + 1, LEAF):
            total = low[i, j] * inv[j, j]
            for k in range(j + 1, i):
                total = total + low[i, k] * inv[k, j]
            inv[i, j] = -total * inv[i, i]
    return inv


def factor_panel(block):
    sub = lax.broadcasted_iota(jnp.int32, (LEAF, 128), 0)
    tiles = [block[LEAF * q : LEAF * (q + 1), :] for q in range(PANEL // LEAF)]
    count = len(tiles)
    for q in range(count):
        inv = leaf_inverse(tiles[q], LEAF * q)
        scaled = jnp.zeros((LEAF, 128), F32)
        for j in range(LEAF):
            column = inv[LEAF - 1, j]
            for i in range(LEAF - 2, j - 1, -1):
                column = jnp.where(sub == i, inv[i, j], column)
            if j:
                column = jnp.where(sub < j, 0.0, column)
            scaled = scaled + column * jnp.broadcast_to(tiles[q][j : j + 1, :], (LEAF, 128))
        raw = {}
        for s in range(q + 1, count):
            for j in range(LEAF):
                lane = LEAF * q + j
                raw[s, j] = jnp.broadcast_to(tiles[s][:, lane : lane + 1], (LEAF, 128))
        for s in range(q + 1, count):
            value = tiles[s]
            for j in range(LEAF):
                factor = raw[s, 0] * inv[j, 0]
                for k in range(1, j + 1):
                    factor = factor + raw[s, k] * inv[j, k]
                value = value - factor * jnp.broadcast_to(scaled[j : j + 1, :], (LEAF, 128))
            tiles[s] = value
        tiles[q] = scaled
    return jnp.concatenate(tiles, axis=0)


def factor_step(k, work, inverse):
    rank = work.shape[0]
    rows = pl.ds(pl.multiple_of(k * PANEL, PANEL), PANEL)
    panel = work[rows, :]
    turned = pltpu.roll(panel[:, :rank], lax.rem(rank - k * PANEL, rank), 1)[:, :128]
    lane = lax.broadcasted_iota(jnp.int32, (PANEL, 128), 1)
    sub = lax.broadcasted_iota(jnp.int32, (PANEL, 128), 0)
    block = jnp.where(lane < PANEL, turned, jnp.where(lane == sub + PANEL, 1.0, 0.0))
    small = factor_panel(block)[:, PANEL : 2 * PANEL]
    done = dot_f32(small, panel)
    inverse[rows, :] = done[:, rank:]
    work[...] = work[...] - rank_update(done[:, :rank], done)


def factor_init(gram, work):
    rank = gram.shape[0]
    sub = lax.broadcasted_iota(jnp.int32, (rank, rank), 0)
    lane = lax.broadcasted_iota(jnp.int32, (rank, rank), 1)
    work[:, :rank] = gram
    work[:, rank:] = jnp.where(sub == lane, 1.0, 0.0)


def kernel(
    n_sa, n_sb, pieces,
    x_hbm, omega_ref, hi_out, lo_out, cross_out, inverse,
    x_v, hi_v, lo_v, hit_v, lot_v, om_v, hh_v, hl_v, gram_v, cross_v,
    gbuf, zbuf, gfull, pairbuf, cbuf, cpart, czbuf, cfull, work,
    x_sem, out_sem, send_sem, recv_sem,
):
    rows, features = x_hbm.shape
    rank = omega_ref.shape[1]
    share = rank // n_sa
    half = rank // 2
    chips = n_sa // 2
    wide = features // pieces
    per_tile = n_sb // (share // 8)
    width = wide // per_tile
    gain = (3.0 / (20.0 * features)) ** 0.5
    chunks = rows // CHUNK
    a_me, b_me = lax.axis_index("sa"), lax.axis_index("sb")
    chip, core = lax.div(a_me, 2), lax.rem(a_me, 2)

    def chunk(i):
        return pl.ds(pl.multiple_of(i * CHUNK, CHUNK), CHUNK)

    def x_copy(i):
        return pltpu.make_async_copy(x_hbm.at[chunk(i)], x_v.at[chunk(i)], x_sem.at[i])

    for i in range(chunks):
        x_copy(i).start()

    def start(phase, axis, count, me, source, target, device=lambda t: t):
        copies = []
        for p in range(1, count):
            peer = lax.rem(me + p, count)
            copy = pltpu.make_async_remote_copy(
                src_ref=source(peer),
                dst_ref=target,
                send_sem=send_sem.at[phase, p],
                recv_sem=recv_sem.at[phase, p],
                device_id={axis: device(peer)},
                device_id_type=pl.DeviceIdType.MESH,
            )
            copy.start()
            copies.append(copy)
        return copies

    def finish(copies):
        for copy in copies:
            copy.wait()

    barrier = pltpu.get_barrier_semaphore()
    for p in range(1, n_sa):
        pl.semaphore_signal(
            barrier, inc=1, device_id={"sa": lax.rem(a_me + p, n_sa)}, device_id_type=pl.DeviceIdType.MESH
        )
    for p in range(1, n_sb):
        pl.semaphore_signal(
            barrier, inc=1, device_id={"sb": lax.rem(b_me + p, n_sb)}, device_id_type=pl.DeviceIdType.MESH
        )

    om_v[...] = omega_ref[...].astype(F32).astype(BF16)
    hh_v[...] = jnp.zeros_like(hh_v)
    hl_v[...] = jnp.zeros_like(hl_v)

    @pl.loop(0, chunks)
    def _(i):
        x_copy(i).wait()
        part = chunk(i)
        sketch = dot(x_v[part, :], om_v[...]) * gain
        hi, lo = split2(sketch)
        hi_t, lo_t = split2(sketch.T)
        hi_v[part, :] = hi
        lo_v[part, :] = lo
        hit_v[:, part] = hi_t
        lot_v[:, part] = lo_t
        hh_v[...] += dot(hi_t, hi)
        hl_v[...] += dot(hi_t, lo)

    outs = [
        pltpu.make_async_copy(hi_v, hi_out, out_sem.at[0]),
        pltpu.make_async_copy(lo_v, lo_out, out_sem.at[1]),
    ]
    for copy in outs:
        copy.start()

    def cut(i):
        return pl.ds(pl.multiple_of(i * share, share), share)

    def total(buffer, count):
        value = buffer[0]
        for i in range(1, count):
            value = value + buffer[i]
        return value

    gram_v[...] = hh_v[...] + (hl_v[...] + hl_v[...].T)
    pl.semaphore_wait(barrier, n_sa - 1 + n_sb - 1)
    gram_copies = start(0, "sa", n_sa, a_me, lambda t: gram_v.at[cut(t)], gbuf.at[a_me])
    gbuf[a_me] = gram_v[cut(a_me), :]

    def half_of(c):
        return pl.ds(pl.multiple_of(c * half, half), half)

    def owned(t):
        first = core * half + t * share
        return pl.ds(pl.multiple_of(first, share), share)

    mine = owned(chip)

    def spot(t, first):
        return (
            pl.ds(pl.multiple_of(first + lax.div(t, per_tile) * 8, 8), 8),
            pl.ds(pl.multiple_of(lax.rem(t, per_tile) * width, width), width),
        )

    def same_core(t):
        return 2 * t + core

    def stages(h):
        base = 3 + 6 * h
        product, full = cross_v.at[h], cfull.at[h]

        def compute():
            for block in range(h * wide, (h + 1) * wide, COLS):
                x = x_v[:, block : block + COLS]
                part = slice(block - h * wide, block - h * wide + COLS)
                cross_v[h, :, part] = dot(hit_v[...], x) + dot(lot_v[...], x)
            return start(
                base, "sa", 2, core, lambda t: product.at[half_of(t)], pairbuf.at[h], lambda t: 2 * chip + t
            )

        def plane_sum():
            cross_v[h, half_of(core), :] += pairbuf[h]
            copies = start(
                base + 1, "sa", chips, chip, lambda t: product.at[owned(t)], cbuf.at[h, chip], same_core
            )
            cbuf[h, chip] = cross_v[h, mine, :]
            return copies

        def z_sum():
            cpart[h] = total(cbuf.at[h], chips)
            copies = start(
                base + 2, "sb", n_sb, b_me, lambda t: cpart.at[h].at[spot(t, 0)], czbuf.at[h, b_me]
            )
            czbuf[h, b_me] = cpart.at[h][spot(b_me, 0)]
            return copies

        def z_gather():
            place = spot(b_me, core * half + chip * share)
            full[place] = total(czbuf.at[h], n_sb)
            return start(base + 3, "sb", n_sb, b_me, lambda t: full.at[place], full.at[place])

        def plane_gather():
            return start(base + 4, "sa", chips, chip, lambda t: full.at[mine], full.at[mine], same_core)

        def pair_gather():
            held = full.at[half_of(core)]
            return start(base + 5, "sa", 2, core, lambda t: held, held, lambda t: 2 * chip + t)

        return [compute, plane_sum, z_sum, z_gather, plane_gather, pair_gather]

    plan = [stages(h) for h in range(pieces)]
    flight = [[] for _ in range(pieces)]

    def advance(stage, *which):
        for h in which or range(pieces):
            if h < pieces:
                finish(flight[h])
                flight[h] = plan[h][stage]()

    panels = rank // PANEL

    def factor(begin, end):
        @pl.loop(begin, end)
        def _(k):
            factor_step(k, work, inverse)

    advance(0, 0)
    finish(gram_copies)
    zbuf[b_me] = total(gbuf, n_sa)
    gram_copies = start(1, "sb", n_sb, b_me, lambda t: zbuf.at[b_me], zbuf.at[b_me])
    advance(1, 0)
    advance(0, 1)
    finish(gram_copies)
    gfull[cut(a_me), :] = total(zbuf, n_sb)
    gram_copies = start(2, "sa", n_sa, a_me, lambda t: gfull.at[cut(a_me)], gfull.at[cut(a_me)])
    advance(1, 1)
    advance(2, 0)
    finish(gram_copies)
    factor_init(gfull[...], work)
    factor(0, 1)
    advance(2, 1)
    advance(3, 0)
    factor(1, 3)
    advance(3, 1)
    advance(4, 0)
    factor(3, 5)
    advance(4, 1)
    factor(5, 6)
    advance(5, 0)
    factor(6, panels)
    advance(5, 1)
    for h in range(pieces):
        finish(flight[h])
        outs.append(
            pltpu.make_async_copy(
                cfull.at[h], cross_out.at[:, pl.ds(h * wide, wide)], out_sem.at[2 + h]
            )
        )
        outs[-1].start()
    for copy in outs:
        copy.wait()


def finish_kernel(total_rows, hi_ref, lo_ref, inverse_ref, cross_ref, basis_ref, proj_ref):
    root = float(total_rows) ** 0.5
    inv_hi, inv_lo = split2(inverse_ref[...])
    hi = hi_ref[...]
    value = dot(hi, inv_hi, 1, 1) + (dot(hi, inv_lo, 1, 1) + dot(lo_ref[...], inv_hi, 1, 1))
    basis_ref[...] = (value * root).astype(BF16)
    c_hi, c_lo = split2(cross_ref[...])
    proj_ref[...] = (dot(inv_hi, c_hi) + (dot(inv_hi, c_lo) + dot(inv_lo, c_hi))) * (root / total_rows)


def on_device(spectra, omega):
    rows, features = spectra.shape
    rank = omega.shape[1]
    n_sa, n_sb = lax.axis_size("sa"), lax.axis_size("sb")
    share = rank // n_sa
    width = features * (share // 8) // n_sb
    pieces = min(2, width // 128)
    wide = features // pieces
    vmem = pltpu.VMEM
    hi, lo, cross, inverse = pl.pallas_call(
        functools.partial(kernel, n_sa, n_sb, pieces),
        out_shape=(
            jax.ShapeDtypeStruct((rows, rank), BF16),
            jax.ShapeDtypeStruct((rows, rank), BF16),
            jax.ShapeDtypeStruct((rank, features), F32),
            jax.ShapeDtypeStruct((rank, rank), F32),
        ),
        in_specs=[pl.BlockSpec(memory_space=pl.ANY), pl.BlockSpec(memory_space=pltpu.VMEM)],
        out_specs=(
            pl.BlockSpec(memory_space=pl.ANY),
            pl.BlockSpec(memory_space=pl.ANY),
            pl.BlockSpec(memory_space=pl.ANY),
            pl.BlockSpec(memory_space=pltpu.VMEM),
        ),
        scratch_shapes=[
            vmem((rows, features), BF16),
            vmem((rows, rank), BF16),
            vmem((rows, rank), BF16),
            vmem((rank, rows), BF16),
            vmem((rank, rows), BF16),
            vmem((features, rank), BF16),
            vmem((rank, rank), F32),
            vmem((rank, rank), F32),
            vmem((rank, rank), F32),
            vmem((pieces, rank, wide), F32),
            vmem((n_sa, share, rank), F32),
            vmem((n_sb, share, rank), F32),
            vmem((rank, rank), F32),
            vmem((pieces, rank // 2, wide), F32),
            vmem((pieces, n_sa // 2, share, wide), F32),
            vmem((pieces, share, wide), F32),
            vmem((pieces, n_sb, 8, width // pieces), F32),
            vmem((pieces, rank, wide), F32),
            vmem((rank, 2 * rank), F32),
            pltpu.SemaphoreType.DMA((rows // CHUNK,)),
            pltpu.SemaphoreType.DMA((2 + pieces,)),
            pltpu.SemaphoreType.DMA((3 + 6 * pieces, max(n_sa, n_sb))),
            pltpu.SemaphoreType.DMA((3 + 6 * pieces, max(n_sa, n_sb))),
        ],
        compiler_params=pltpu.CompilerParams(
            collective_id=0, has_side_effects=True, vmem_limit_bytes=52 * 2**20
        ),
    )(spectra, omega)
    steps = 4
    tall, slim = rows // steps, features // steps
    return pl.pallas_call(
        functools.partial(finish_kernel, rows * n_sa * n_sb),
        grid=(steps,),
        out_shape=(
            jax.ShapeDtypeStruct((rows, rank), BF16),
            jax.ShapeDtypeStruct((rank, features), F32),
        ),
        in_specs=[
            pl.BlockSpec((tall, rank), lambda i: (i, 0)),
            pl.BlockSpec((tall, rank), lambda i: (i, 0)),
            pl.BlockSpec((rank, rank), lambda i: (0, 0)),
            pl.BlockSpec((rank, slim), lambda i: (0, i)),
        ],
        out_specs=(
            pl.BlockSpec((tall, rank), lambda i: (i, 0)),
            pl.BlockSpec((rank, slim), lambda i: (0, i)),
        ),
        compiler_params=pltpu.CompilerParams(vmem_limit_bytes=40 * 2**20),
    )(hi, lo, inverse, cross)


def solution(mesh):
    return jax.shard_map(
        on_device,
        mesh=mesh,
        in_specs=(P(("sa", "sb"), None), P()),
        out_specs=(P(("sa", "sb"), None), P()),
        check_vma=False,
    )
```

```python
import functools

import jax
import jax.numpy as jnp
from jax import lax
from jax.experimental import pallas as pl
from jax.experimental.pallas import tpu as pltpu
from jax.sharding import PartitionSpec as P

F32 = jnp.float32
BF16 = jnp.bfloat16
PANEL = 32
LEAF = 8
CHUNK = 1024
COLS = 256


def dot(a, b, ca=1, cb=0):
    return lax.dot_general(a, b, (((ca,), (cb,)), ((), ())), preferred_element_type=F32)


def split2(a):
    high = a.astype(BF16)
    return high, (a - high.astype(F32)).astype(BF16)


def split3(a):
    high, rest = a.astype(BF16), None
    rest = a - high.astype(F32)
    mid = rest.astype(BF16)
    return high, mid, (rest - mid.astype(F32)).astype(BF16)


def dot_f32(a, b):
    a1, a2, a3 = split3(a)
    b1, b2, b3 = split3(b)
    return dot(
        jnp.concatenate([a1, a1, a1, a2, a2, a3], axis=1),
        jnp.concatenate([b1, b2, b3, b1, b2, b1], axis=0),
    )


def rank_update(u, v):
    a1, a2, a3 = split3(u)
    b1, b2, b3 = split3(v)
    return dot(
        jnp.concatenate([a1, a1, a1, a2, a2, a3], axis=0),
        jnp.concatenate([b1, b2, b3, b1, b2, b1], axis=0),
        0,
        0,
    )


def leaf_inverse(block, first):
    a = {}
    for j in range(LEAF):
        column = jnp.broadcast_to(block[:, first + j : first + j + 1], (LEAF, 128))
        for i in range(j, LEAF):
            a[i, j] = jnp.broadcast_to(column[i : i + 1, :], (LEAF, 128))
    low, inv = {}, {}
    for j in range(LEAF):
        inv[j, j] = lax.rsqrt(a[j, j])
        for i in range(j + 1, LEAF):
            low[i, j] = a[i, j] * inv[j, j]
        for k in range(j + 1, LEAF):
            for i in range(k, LEAF):
                a[i, k] = a[i, k] - low[i, j] * low[k, j]
    for j in range(LEAF):
        for i in range(j + 1, LEAF):
            total = low[i, j] * inv[j, j]
            for k in range(j + 1, i):
                total = total + low[i, k] * inv[k, j]
            inv[i, j] = -total * inv[i, i]
    return inv


def factor_panel(block):
    sub = lax.broadcasted_iota(jnp.int32, (LEAF, 128), 0)
    tiles = [block[LEAF * q : LEAF * (q + 1), :] for q in range(PANEL // LEAF)]
    count = len(tiles)
    for q in range(count):
        inv = leaf_inverse(tiles[q], LEAF * q)
        scaled = jnp.zeros((LEAF, 128), F32)
        for j in range(LEAF):
            column = inv[LEAF - 1, j]
            for i in range(LEAF - 2, j - 1, -1):
                column = jnp.where(sub == i, inv[i, j], column)
            if j:
                column = jnp.where(sub < j, 0.0, column)
            scaled = scaled + column * jnp.broadcast_to(tiles[q][j : j + 1, :], (LEAF, 128))
        raw = {}
        for s in range(q + 1, count):
            for j in range(LEAF):
                lane = LEAF * q + j
                raw[s, j] = jnp.broadcast_to(tiles[s][:, lane : lane + 1], (LEAF, 128))
        for s in range(q + 1, count):
            value = tiles[s]
            for j in range(LEAF):
                factor = raw[s, 0] * inv[j, 0]
                for k in range(1, j + 1):
                    factor = factor + raw[s, k] * inv[j, k]
                value = value - factor * jnp.broadcast_to(scaled[j : j + 1, :], (LEAF, 128))
            tiles[s] = value
        tiles[q] = scaled
    return jnp.concatenate(tiles, axis=0)


def factor_step(k, work, inverse):
    rank = work.shape[0]
    rows = pl.ds(pl.multiple_of(k * PANEL, PANEL), PANEL)
    panel = work[rows, :]
    turned = pltpu.roll(panel[:, :rank], lax.rem(rank - k * PANEL, rank), 1)[:, :128]
    lane = lax.broadcasted_iota(jnp.int32, (PANEL, 128), 1)
    sub = lax.broadcasted_iota(jnp.int32, (PANEL, 128), 0)
    block = jnp.where(lane < PANEL, turned, jnp.where(lane == sub + PANEL, 1.0, 0.0))
    small = factor_panel(block)[:, PANEL : 2 * PANEL]
    done = dot_f32(small, panel)
    inverse[rows, :] = done[:, rank:]
    work[...] = work[...] - rank_update(done[:, :rank], done)


def factor_init(gram, work):
    rank = gram.shape[0]
    sub = lax.broadcasted_iota(jnp.int32, (rank, rank), 0)
    lane = lax.broadcasted_iota(jnp.int32, (rank, rank), 1)
    work[:, :rank] = gram
    work[:, rank:] = jnp.where(sub == lane, 1.0, 0.0)


def kernel(
    n_sa, n_sb, pieces,
    x_hbm, omega_ref, basis_out, proj_ref,
    x_v, hi_v, lo_v, both_v, om_v, grams_v, gram_v, cross_v,
    gbuf, zbuf, gfull, pairbuf, cbuf, cpart, czbuf, cfull, work, inverse, basis_v,
    x_sem, out_sem, send_sem, recv_sem,
):
    rows, features = x_hbm.shape
    rank = omega_ref.shape[1]
    share = rank // n_sa
    half = rank // 2
    chips = n_sa // 2
    wide = features // pieces
    per_tile = n_sb // (share // 8)
    width = wide // per_tile
    gain = (3.0 / (20.0 * features)) ** 0.5
    chunks = rows // CHUNK
    a_me, b_me = lax.axis_index("sa"), lax.axis_index("sb")
    chip, core = lax.div(a_me, 2), lax.rem(a_me, 2)

    def chunk(i):
        return pl.ds(pl.multiple_of(i * CHUNK, CHUNK), CHUNK)

    def x_copy(i):
        return pltpu.make_async_copy(x_hbm.at[chunk(i)], x_v.at[chunk(i)], x_sem.at[i])

    for i in range(chunks):
        x_copy(i).start()

    def start(phase, axis, count, me, source, target, device=lambda t: t):
        copies = []
        for p in range(1, count):
            peer = lax.rem(me + p, count)
            copy = pltpu.make_async_remote_copy(
                src_ref=source(peer),
                dst_ref=target,
                send_sem=send_sem.at[phase, p],
                recv_sem=recv_sem.at[phase, p],
                device_id={axis: device(peer)},
                device_id_type=pl.DeviceIdType.MESH,
            )
            copy.start()
            copies.append(copy)
        return copies

    def finish(copies):
        for copy in copies:
            copy.wait()

    barrier = pltpu.get_barrier_semaphore()
    for p in range(1, n_sa):
        pl.semaphore_signal(
            barrier, inc=1, device_id={"sa": lax.rem(a_me + p, n_sa)}, device_id_type=pl.DeviceIdType.MESH
        )
    for p in range(1, n_sb):
        pl.semaphore_signal(
            barrier, inc=1, device_id={"sb": lax.rem(b_me + p, n_sb)}, device_id_type=pl.DeviceIdType.MESH
        )

    om_v[...] = omega_ref[...].astype(F32).astype(BF16)
    grams_v[...] = jnp.zeros_like(grams_v)

    @pl.loop(0, chunks)
    def _(i):
        x_copy(i).wait()
        part = chunk(i)
        sketch = dot(x_v[part, :], om_v[...]) * gain
        hi, lo = split2(sketch)
        hi_t, lo_t = split2(sketch.T)
        hi_v[part, :] = hi
        lo_v[part, :] = lo
        both_t = jnp.concatenate([hi_t, lo_t], axis=0)
        both_v[:, part] = both_t
        grams_v[...] += dot(both_t, hi)

    def cut(i):
        return pl.ds(pl.multiple_of(i * share, share), share)

    def total(buffer, count):
        value = buffer[0]
        for i in range(1, count):
            value = value + buffer[i]
        return value

    small = grams_v[rank:, :]
    gram_v[...] = grams_v[:rank, :] + (small + small.T)
    pl.semaphore_wait(barrier, n_sa - 1 + n_sb - 1)
    gram_copies = start(0, "sa", n_sa, a_me, lambda t: gram_v.at[cut(t)], gbuf.at[a_me])
    gbuf[a_me] = gram_v[cut(a_me), :]

    def half_of(c):
        return pl.ds(pl.multiple_of(c * half, half), half)

    def owned(t):
        first = core * half + t * share
        return pl.ds(pl.multiple_of(first, share), share)

    mine = owned(chip)

    def spot(t, first):
        return (
            pl.ds(pl.multiple_of(first + lax.div(t, per_tile) * 8, 8), 8),
            pl.ds(pl.multiple_of(lax.rem(t, per_tile) * width, width), width),
        )

    def same_core(t):
        return 2 * t + core

    def stages(h):
        base = 3 + 6 * h
        product, full = cross_v.at[h], cfull.at[h]

        def compute():
            for block in range(h * wide, (h + 1) * wide, COLS):
                x = x_v[:, block : block + COLS]
                part = slice(block - h * wide, block - h * wide + COLS)
                both = dot(both_v[...], x)
                cross_v[h, :, part] = both[:rank] + both[rank:]
            return start(
                base, "sa", 2, core, lambda t: product.at[half_of(t)], pairbuf.at[h], lambda t: 2 * chip + t
            )

        def plane_sum():
            cross_v[h, half_of(core), :] += pairbuf[h]
            copies = start(
                base + 1, "sa", chips, chip, lambda t: product.at[owned(t)], cbuf.at[h, chip], same_core
            )
            cbuf[h, chip] = cross_v[h, mine, :]
            return copies

        def z_sum():
            cpart[h] = total(cbuf.at[h], chips)
            copies = start(
                base + 2, "sb", n_sb, b_me, lambda t: cpart.at[h].at[spot(t, 0)], czbuf.at[h, b_me]
            )
            czbuf[h, b_me] = cpart.at[h][spot(b_me, 0)]
            return copies

        def z_gather():
            place = spot(b_me, core * half + chip * share)
            full[place] = total(czbuf.at[h], n_sb)
            return start(base + 3, "sb", n_sb, b_me, lambda t: full.at[place], full.at[place])

        def plane_gather():
            return start(base + 4, "sa", chips, chip, lambda t: full.at[mine], full.at[mine], same_core)

        def pair_gather():
            held = full.at[half_of(core)]
            return start(base + 5, "sa", 2, core, lambda t: held, held, lambda t: 2 * chip + t)

        return [compute, plane_sum, z_sum, z_gather, plane_gather, pair_gather]

    plan = [stages(h) for h in range(pieces)]
    flight = [[] for _ in range(pieces)]

    def advance(stage, *which):
        for h in which or range(pieces):
            if h < pieces:
                finish(flight[h])
                flight[h] = plan[h][stage]()

    panels = rank // PANEL

    def factor(begin, end):
        @pl.loop(begin, end)
        def _(k):
            factor_step(k, work, inverse)

    advance(0)
    finish(gram_copies)
    zbuf[b_me] = total(gbuf, n_sa)
    gram_copies = start(1, "sb", n_sb, b_me, lambda t: zbuf.at[b_me], zbuf.at[b_me])
    advance(1)
    finish(gram_copies)
    gfull[cut(a_me), :] = total(zbuf, n_sb)
    gram_copies = start(2, "sa", n_sa, a_me, lambda t: gfull.at[cut(a_me)], gfull.at[cut(a_me)])
    advance(2, 0)
    finish(gram_copies)
    factor_init(gfull[...], work)
    factor(0, 1)
    advance(2, 1)
    advance(3, 0)
    factor(1, 3)
    advance(3, 1)
    advance(4, 0)
    factor(3, 5)
    advance(4, 1)
    factor(5, 6)
    advance(5, 0)
    factor(6, panels)
    root = float(rows * n_sa * n_sb) ** 0.5
    inv_hi, inv_lo = split2(inverse[...])

    def basis_copy(i):
        return pltpu.make_async_copy(basis_v.at[chunk(i)], basis_out.at[chunk(i)], out_sem.at[i])

    @pl.loop(0, chunks)
    def _(i):
        hi = hi_v[chunk(i), :]
        value = dot(hi, inv_hi, 1, 1) + (dot(hi, inv_lo, 1, 1) + dot(lo_v[chunk(i), :], inv_hi, 1, 1))
        basis_v[chunk(i), :] = (value * root).astype(BF16)
        basis_copy(i).start()

    advance(5, 1)
    scale = root / (rows * n_sa * n_sb)
    for h in range(pieces):
        finish(flight[h])
        c_hi, c_lo = split2(cfull[h])
        proj_ref[:, h * wide : (h + 1) * wide] = (
            dot(inv_hi, c_hi) + (dot(inv_hi, c_lo) + dot(inv_lo, c_hi))
        ) * scale
    for i in range(chunks):
        basis_copy(i).wait()


def on_device(spectra, omega):
    rows, features = spectra.shape
    rank = omega.shape[1]
    n_sa, n_sb = lax.axis_size("sa"), lax.axis_size("sb")
    share = rank // n_sa
    width = features * (share // 8) // n_sb
    pieces = min(2, width // 128)
    wide = features // pieces
    vmem = pltpu.VMEM
    return pl.pallas_call(
        functools.partial(kernel, n_sa, n_sb, pieces),
        out_shape=(
            jax.ShapeDtypeStruct((rows, rank), BF16),
            jax.ShapeDtypeStruct((rank, features), F32),
        ),
        in_specs=[pl.BlockSpec(memory_space=pl.ANY), pl.BlockSpec(memory_space=pltpu.VMEM)],
        out_specs=(
            pl.BlockSpec(memory_space=pl.ANY),
            pl.BlockSpec(memory_space=pltpu.VMEM),
        ),
        scratch_shapes=[
            vmem((rows, features), BF16),
            vmem((rows, rank), BF16),
            vmem((rows, rank), BF16),
            vmem((2 * rank, rows), BF16),
            vmem((features, rank), BF16),
            vmem((2 * rank, rank), F32),
            vmem((rank, rank), F32),
            vmem((pieces, rank, wide), F32),
            vmem((n_sa, share, rank), F32),
            vmem((n_sb, share, rank), F32),
            vmem((rank, rank), F32),
            vmem((pieces, rank // 2, wide), F32),
            vmem((pieces, n_sa // 2, share, wide), F32),
            vmem((pieces, share, wide), F32),
            vmem((pieces, n_sb, 8, width // pieces), F32),
            vmem((pieces, rank, wide), F32),
            vmem((rank, 2 * rank), F32),
            vmem((rank, rank), F32),
            vmem((rows, rank), BF16),
            pltpu.SemaphoreType.DMA((rows // CHUNK,)),
            pltpu.SemaphoreType.DMA((rows // CHUNK,)),
            pltpu.SemaphoreType.DMA((3 + 6 * pieces, max(n_sa, n_sb))),
            pltpu.SemaphoreType.DMA((3 + 6 * pieces, max(n_sa, n_sb))),
        ],
        compiler_params=pltpu.CompilerParams(
            collective_id=0, has_side_effects=True, vmem_limit_bytes=52 * 2**20
        ),
    )(spectra, omega)


def solution(mesh):
    return jax.shard_map(
        on_device,
        mesh=mesh,
        in_specs=(P(("sa", "sb"), None), P()),
        out_specs=(P(("sa", "sb"), None), P()),
        check_vma=False,
    )
```
